32 devices in a mesh: gx: 4 (over y, x), gy: 4 (over z), gz: 2 (over core).
Axes of the slice: x: 2, y: 2, z: 4, core: 2. Of those that a mesh axis runs over, the one named last changes fastest.
Arguments:
- positions: float32 [3, 4, 8, 2, 128], P(None, 'gx', 'gy', 'gz'), may hold values from 0 to 80, as said below
- species: int32 [4, 8, 2, 128], P('gx', 'gy', 'gz'), may hold values from -1 to 7, as said below
- neighbours: int32 [8, 4, 8, 2, 128], P(None, 'gx', 'gy', 'gz'), may hold values from -1 to 3455, as said below
- embed: bfloat16 [128, 8], replicated, may hold values from -6 to 6
- radial_in: bfloat16 [2, 64, 8], replicated, may hold values from -2 to 2
- radial_mid: bfloat16 [2, 64, 64], replicated, may hold values from -0.75 to 0.75
- radial_out: bfloat16 [2, 256, 64], replicated, may hold values from -0.75 to 0.75
- message: bfloat16 [2, 128, 128], replicated, may hold values from -0.5 to 0.5
- mixing: float32 [2, 384, 8], replicated, may hold values from -15 to 15
- update: bfloat16 [2, 128, 384], replicated, may hold values from -0.3125 to 0.3125
- readout_linear: float32 [128], replicated, may hold values from -0.5 to 0.5
- readout_hidden: bfloat16 [16, 128], replicated, may hold values from -0.5 to 0.5
- readout_out: float32 [16], replicated, may hold values from -4 to 4
- charge_proj: bfloat16 [4, 128], replicated, may hold values from -1 to 1
Outputs:
- atom_energy: float32 [4, 8, 2, 128], P('gx', 'gy', 'gz')
- forces: float32 [3, 4, 8, 2, 128], P(None, 'gx', 'gy', 'gz')
The draws below stay inside these ranges and needn't reach their ends.
Inputs may be any that keep to these rules, and one draw needn't show every extreme that they name: `species`: -1 marks an empty slot; in every cell the occupied slots come first. `neighbours`: an entry e other than -1 names row e % 128 of the cell displaced from the atom's cell by (e // 128 // 9 - 1, e // 128 // 3 % 3 - 1, e // 128 % 3 - 1); that cell lies in the grid, that slot is occupied and is not the atom itself; entries other than -1 come first; empty slots hold only -1. `positions`: components 0, 1, 2 of a slot in cell (a, b, c) lie in [10 a, 10 a + 10), [10 b, 10 b + 10) and [10 c, 10 c + 10).
All inputs are finite; a program needn't handle non-finite values.
Results may differ from the reference program's by a relative error of at most 0.022.
Values may be sent and summed in bfloat16 or wider, within the bound.
A program may use at most 128 MiB of HBM per device.

```python
import math
import jax
import jax.numpy as jnp
from jax import lax

C = 128
NB = 8
RH = 64
RO = 16
NS = 8
NQ = 4
K = 8
ROWS = 128
KX = 8
KY = 8
KZ = 4
XC = 4
YC = 8
ZC = 2


def cell_counts(key):
    base_key = jax.random.fold_in(key, 11)
    dense_fill = jax.random.randint(jax.random.fold_in(base_key, 1), (XC, YC, ZC), ROWS * 3 // 4, ROWS + 1)
    sparse_fill = jax.random.randint(jax.random.fold_in(base_key, 2), (XC, YC, ZC), max(2, ROWS // 16), ROWS * 3 // 8 + 1)
    layer_index = jnp.arange(ZC)[None, None, :]
    return jnp.where(layer_index < ZC // 2, dense_fill, sparse_fill).astype(jnp.int32)


def draw_species(key, part):
    counts_grid = cell_counts(key)
    kind_draw = jax.random.randint(jax.random.fold_in(key, 21), (XC, YC, ZC, ROWS), 0, NS)
    slot_index = jnp.arange(ROWS)[None, None, None, :]
    return jnp.where(slot_index < counts_grid[..., None], kind_draw, -1).astype(jnp.int32)


def draw_neighbours(key, part):
    counts_grid = cell_counts(key)
    full_shape = (K, XC, YC, ZC, ROWS)
    index_x = jnp.broadcast_to(jnp.arange(XC)[None, :, None, None, None], full_shape)
    index_y = jnp.broadcast_to(jnp.arange(YC)[None, None, :, None, None], full_shape)
    index_z = jnp.broadcast_to(jnp.arange(ZC)[None, None, None, :, None], full_shape)
    shift_x = jax.random.randint(jax.random.fold_in(key, 31), full_shape, -1, 2)
    shift_y = jax.random.randint(jax.random.fold_in(key, 32), full_shape, -1, 2)
    shift_z = jax.random.randint(jax.random.fold_in(key, 33), full_shape, -1, 2)
    shift_x = jnp.where((index_x + shift_x < 0) | (index_x + shift_x >= XC), 0, shift_x)
    shift_y = jnp.where((index_y + shift_y < 0) | (index_y + shift_y >= YC), 0, shift_y)
    shift_z = jnp.where((index_z + shift_z < 0) | (index_z + shift_z >= ZC), 0, shift_z)
    near_count = counts_grid[index_x + shift_x, index_y + shift_y, index_z + shift_z]
    partner_row = jax.random.randint(jax.random.fold_in(key, 34), full_shape, 0, near_count)
    slot_index = jnp.broadcast_to(jnp.arange(ROWS)[None, None, None, None, :], full_shape)
    itself = (shift_x == 0) & (shift_y == 0) & (shift_z == 0) & (partner_row == slot_index)
    partner_row = jnp.where(itself, (partner_row + 1) % near_count, partner_row)
    dense_degree = jax.random.randint(jax.random.fold_in(key, 35), (XC, YC, ZC, ROWS), K // 2, K + 1)
    sparse_degree = jax.random.randint(jax.random.fold_in(key, 36), (XC, YC, ZC, ROWS), K // 4, K // 2 + 1)
    layer_index = jnp.arange(ZC)[None, None, :, None]
    degree = jnp.where(layer_index < ZC // 2, dense_degree, sparse_degree)
    slot_k = jnp.arange(K)[:, None, None, None, None]
    own_count = counts_grid[None, :, :, :, None]
    live_slot = (slot_k < degree[None]) & (slot_index < own_count)
    cell_code = (shift_x + 1) * 9 + (shift_y + 1) * 3 + (shift_z + 1)
    return jnp.where(live_slot, cell_code * ROWS + partner_row, -1).astype(jnp.int32)


def draw_positions(key, part):
    full_shape = (XC, YC, ZC, ROWS)
    fraction = jax.random.uniform(key, (3,) + full_shape, jnp.float32)
    corner_x = jnp.broadcast_to(jnp.arange(XC).astype(jnp.float32)[:, None, None, None], full_shape)
    corner_y = jnp.broadcast_to(jnp.arange(YC).astype(jnp.float32)[None, :, None, None], full_shape)
    corner_z = jnp.broadcast_to(jnp.arange(ZC).astype(jnp.float32)[None, None, :, None], full_shape)
    corner = jnp.stack([corner_x, corner_y, corner_z])
    return ((corner + fraction) * 10.0).astype(jnp.float32)


def gaussian(rng, shape, width, most, kind=jnp.bfloat16):
    drawn = jax.random.normal(rng, shape, jnp.float32) * width
    return jnp.minimum(jnp.maximum(drawn, -most), most).astype(kind)


def setup_inputs(seed: int = 0) -> dict:
    splits = jax.random.split(jax.random.key(seed), 15)
    return {
        "positions": draw_positions(jax.random.fold_in(splits[14], 71), 0),
        "species": draw_species(jax.random.fold_in(splits[14], 71), 0),
        "neighbours": draw_neighbours(jax.random.fold_in(splits[14], 71), 0),
        "embed": gaussian(splits[3], (C, NS), 1.0, 6.0),
        "radial_in": gaussian(splits[4], (2, RH, NB), NB ** -0.5, 2.0),
        "radial_mid": gaussian(splits[5], (2, RH, RH), RH ** -0.5, 0.75),
        "radial_out": gaussian(splits[6], (2, 2 * C, RH), RH ** -0.5, 0.75),
        "message": gaussian(splits[7], (2, C, C), C ** -0.5, 0.5),
        "mixing": gaussian(splits[8], (2, 3 * C, NS), 2.5, 15.0, jnp.float32),
        "update": gaussian(splits[9], (2, C, 3 * C), (3 * C) ** -0.5, 0.3125),
        "readout_linear": gaussian(splits[10], (C,), C ** -0.5, 0.5, jnp.float32),
        "readout_hidden": gaussian(splits[11], (RO, C), C ** -0.5, 0.5),
        "readout_out": gaussian(splits[12], (RO,), 1.0, 4.0, jnp.float32),
        "charge_proj": gaussian(splits[13], (NQ, C), (C // 4) ** -0.5, 1.0),
    }


cell_side_length = 10.0
cutoff = 36.0
sigma = 6.0
soft_core = 1.0

def rounded(values):
    frozen = lax.stop_gradient(values)
    snapped = lax.optimization_barrier(frozen.astype(jnp.bfloat16)).astype(jnp.float32)
    return values + (snapped - frozen)

def matmul(weights, operand):
    return jnp.dot(weights.astype(jnp.float32), operand, precision=lax.Precision.HIGHEST, preferred_element_type=jnp.float32)

def edge_sums(radial_w, centre, partner_index, live_mask, pos_flat, msg_flat):
    w_first, w_second, w_third = radial_w
    slot_count, count_of_rows = partner_index.shape
    flat_index = partner_index.reshape(-1)
    partner = jnp.take(pos_flat, flat_index, axis=1).reshape(3, slot_count, count_of_rows)
    offset_vec = partner - centre[:, None, :]
    distance = jnp.sqrt(lax.optimization_barrier(jnp.sum(offset_vec * offset_vec, axis=0)) + soft_core)
    reduced = (distance / cutoff).reshape(1, -1)
    harmonic = (jnp.arange(w_first.shape[1]) + 1).astype(jnp.float32)[:, None]
    envelope = (1.0 - reduced * reduced) * (1.0 - reduced * reduced)
    bessel = rounded(jnp.sin(jnp.pi * harmonic * reduced) * envelope)
    hidden_one = rounded(jax.nn.silu(matmul(w_first, bessel)))
    hidden_two = rounded(jax.nn.silu(matmul(w_second, hidden_one)))
    radial = matmul(w_third, hidden_two)
    channels = msg_flat.shape[0]
    incoming = jnp.take(msg_flat, flat_index, axis=1) * live_mask.reshape(1, -1)
    scalar_terms = (radial[:channels] * incoming).reshape(channels, slot_count, count_of_rows)
    vector_terms = (radial[channels:] * incoming).reshape(channels, slot_count, count_of_rows)
    direction = offset_vec / distance[None]
    scalar_sum = lax.optimization_barrier(jnp.sum(scalar_terms, axis=1))
    vector_sum = jnp.einsum('ckr,mkr->mcr', vector_terms, direction, precision=lax.Precision.HIGHEST)
    return (scalar_sum, vector_sum)

def cell_update(radial_w, w_update, node_state, centre, partner_index, live_mask, mixing_cell, pos_flat, msg_flat):
    slot_count = partner_index.shape[0]
    scalar_sum, vector_sum = edge_sums(radial_w, centre, partner_index, live_mask, pos_flat, msg_flat)
    factor = 2.0 / slot_count
    scalar_sum = scalar_sum * factor
    vector_sum = vector_sum * factor
    invariant = jnp.concatenate([scalar_sum, lax.optimization_barrier(jnp.sum(vector_sum * vector_sum, axis=0)), scalar_sum * scalar_sum], axis=0)
    weighted = rounded(invariant * mixing_cell)
    return rounded(node_state + matmul(w_update, weighted))

def run_layer(radial_w, w_update, node_cells, centre_cells, index_cells, live_cells, mixing_cells, pos_flat, msg_flat):

    def one_cell(cell_items):
        return cell_update(radial_w, w_update, cell_items[0], cell_items[1], cell_items[2], cell_items[3], cell_items[4], pos_flat, msg_flat)
    return lax.map(jax.checkpoint(one_cell), (node_cells, centre_cells, index_cells, live_cells, mixing_cells))

def to_cells(grid_values):
    leading = grid_values.shape[0]
    return jnp.moveaxis(grid_values, 0, 3).reshape(-1, leading, grid_values.shape[-1])

def from_cells(cell_values, extent_x, extent_y, extent_z):
    stacked = cell_values.reshape(extent_x, extent_y, extent_z, cell_values.shape[1], cell_values.shape[2])
    return jnp.moveaxis(stacked, 3, 0)

def pad_grid(flat_values, extent_x, extent_y, extent_z, count_of_rows):
    shaped = flat_values.reshape(flat_values.shape[0], extent_x, extent_y, extent_z, count_of_rows)
    padded = jnp.pad(shaped, ((0, 0), (1, 1), (1, 1), (1, 1), (0, 0)))
    return padded.reshape(flat_values.shape[0], -1)

def neighbour_flat(neighbours, extent_y, extent_z, count_of_rows, tag_flat):
    count_along_first, count_along_second, count_along_third = (neighbours.shape[1], neighbours.shape[2], neighbours.shape[3])
    clipped = jnp.maximum(neighbours, 0)
    cell_code = clipped // count_of_rows
    slot_row = clipped % count_of_rows
    shift_x = cell_code // 9 - 1
    shift_y = cell_code // 3 % 3 - 1
    shift_z = cell_code % 3 - 1
    index_x = jnp.arange(count_along_first, dtype=jnp.int32)[None, :, None, None, None]
    index_y = jnp.arange(count_along_second, dtype=jnp.int32)[None, None, :, None, None]
    index_z = jnp.arange(count_along_third, dtype=jnp.int32)[None, None, None, :, None]
    flat_index = (((index_x + 1 + shift_x) * extent_y + index_y + 1 + shift_y) * extent_z + index_z + 1 + shift_z) * count_of_rows + slot_row
    flat_index = flat_index.astype(jnp.int32)
    partner_tag = jnp.take(tag_flat, flat_index.reshape(-1)).reshape(flat_index.shape)
    live_mask = jnp.where((neighbours >= 0) & (partner_tag > 0.0), 1.0, 0.0).astype(jnp.float32)
    return (flat_index, live_mask)

def wave_vector_list(length_along_first, length_along_second, length_along_third, total_slot_count):
    first_wave_grid, second_wave_grid, third_wave_grid = jnp.meshgrid(jnp.arange(KX).astype(jnp.float32), jnp.arange(KY).astype(jnp.float32) - KY // 2, jnp.arange(KZ).astype(jnp.float32) - KZ // 2, indexing='ij')
    first_wave_grid = first_wave_grid.reshape(-1)
    second_wave_grid = second_wave_grid.reshape(-1)
    third_wave_grid = third_wave_grid.reshape(-1)
    reciprocal_vectors = 2.0 * jnp.pi * jnp.stack([first_wave_grid / length_along_first, second_wave_grid / length_along_second, third_wave_grid / length_along_third])
    integer_sq = first_wave_grid * first_wave_grid + second_wave_grid * second_wave_grid + third_wave_grid * third_wave_grid
    wave_squared_norm = lax.optimization_barrier(jnp.sum(reciprocal_vectors * reciprocal_vectors, axis=0))
    reciprocal_weight = jnp.where(integer_sq > 0.0, jnp.exp(-0.5 * sigma * sigma * wave_squared_norm) / jnp.maximum(integer_sq, 1.0), 0.0)
    return (reciprocal_vectors, reciprocal_weight / math.sqrt(total_slot_count))

def reference(positions, species, neighbours, embed, radial_in, radial_mid, radial_out, message, mixing, update, readout_linear, readout_hidden, readout_out, charge_proj):
    channels, kinds = embed.shape
    count_along_first, count_along_second, count_along_third, count_of_rows = species.shape
    tag = (species + 1).astype(jnp.float32)
    tag_padded = jnp.pad(tag, ((1, 1), (1, 1), (1, 1), (0, 0))).reshape(-1)
    flat_index, live_mask = neighbour_flat(neighbours, count_along_second + 2, count_along_third + 2, count_of_rows, tag_padded)
    index_cells = to_cells(flat_index)
    live_cells = to_cells(live_mask)
    kind_ids = (jnp.arange(kinds) + 1).astype(jnp.float32)[:, None]
    onehot = jnp.where(tag.reshape(1, -1) == kind_ids, 1.0, 0.0).astype(jnp.float32)
    initial = matmul(embed, onehot)
    message_one = rounded(matmul(message[0], initial))
    padded_one = pad_grid(message_one, count_along_first, count_along_second, count_along_third, count_of_rows)
    mixing_one = to_cells(matmul(mixing[0], onehot).reshape(-1, count_along_first, count_along_second, count_along_third, count_of_rows))
    mixing_two = to_cells(matmul(mixing[1], onehot).reshape(-1, count_along_first, count_along_second, count_along_third, count_of_rows))
    initial_cells = to_cells(initial.reshape(channels, count_along_first, count_along_second, count_along_third, count_of_rows))
    reciprocal_vectors, reciprocal_weight = wave_vector_list(cell_side_length * count_along_first, cell_side_length * count_along_second, 3.0 * cell_side_length * count_along_third, count_along_first * count_along_second * count_along_third * count_of_rows)

    def energy(atom_coordinates):
        pos_padded = pad_grid(atom_coordinates.reshape(3, -1), count_along_first, count_along_second, count_along_third, count_of_rows)
        centre_cells = to_cells(atom_coordinates)
        layer_one = run_layer((radial_in[0], radial_mid[0], radial_out[0]), update[0], initial_cells, centre_cells, index_cells, live_cells, mixing_one, pos_padded, padded_one)
        state_one = from_cells(layer_one, count_along_first, count_along_second, count_along_third).reshape(channels, -1)
        message_two = rounded(matmul(message[1], state_one))
        padded_two = pad_grid(message_two, count_along_first, count_along_second, count_along_third, count_of_rows)
        layer_two = run_layer((radial_in[1], radial_mid[1], radial_out[1]), update[1], layer_one, centre_cells, index_cells, live_cells, mixing_two, pos_padded, padded_two)
        state_two = from_cells(layer_two, count_along_first, count_along_second, count_along_third).reshape(channels, -1)
        readout_act = jax.nn.silu(matmul(readout_hidden, state_two))
        short_range = jnp.dot(readout_linear, state_one, precision=lax.Precision.HIGHEST) + jnp.dot(readout_out, readout_act, precision=lax.Precision.HIGHEST)
        charge = matmul(charge_proj, state_two)
        phase_angle = jnp.dot(reciprocal_vectors.T, atom_coordinates.reshape(3, -1), precision=lax.Precision.HIGHEST)
        cosine = jnp.cos(phase_angle)
        sine = jnp.sin(phase_angle)
        structure_cos = jnp.dot(cosine, charge.T, precision=lax.Precision.HIGHEST)
        structure_sin = jnp.dot(sine, charge.T, precision=lax.Precision.HIGHEST)
        potential = jnp.dot((structure_cos * reciprocal_weight[:, None]).T, cosine, precision=lax.Precision.HIGHEST)
        potential = potential + jnp.dot((structure_sin * reciprocal_weight[:, None]).T, sine, precision=lax.Precision.HIGHEST)
        per_atom = short_range + lax.optimization_barrier(jnp.sum(charge * potential, axis=0))
        return (jnp.sum(per_atom), per_atom)
    (total_energy, per_atom), gradient = jax.value_and_grad(energy, has_aux=True)(positions)
    return (per_atom.reshape(count_along_first, count_along_second, count_along_third, count_of_rows), -gradient)
```

```python
import functools
import math

import jax
import jax.numpy as jnp
import numpy as np
from jax import lax
from jax.experimental import pallas as pl
from jax.experimental.pallas import tpu as pltpu
from jax.sharding import PartitionSpec as P

KX = 8
KY = 8
KZ = 4
C = 128
RH = 64
NS = 8
NQ = 4
K = 8
ROWS = 128
EDGES = K * ROWS
NEAR = 18
EXT = 24
SLOTS = EXT * ROWS

cell_side_length = 10.0
cutoff = 36.0
sigma = 6.0

MESH = pl.DeviceIdType.MESH
HIGH = lax.Precision.HIGHEST
f32 = jnp.float32
bf16 = jnp.bfloat16
MIRROR_Y = (3, 1, 2, 0)
STEP_Y = (-1, 0, 0, 1)
OWN = (8, 14)


def dot(a, b, dims=((1,), (0,)), precision=None):
    return lax.dot_general(
        a, b, (dims, ((), ())), preferred_element_type=f32, precision=precision
    )


def sigmoid(v):
    return 1.0 / (1.0 + jnp.exp(-v))


def wave_table(total_x, total_y, total_z):
    m2, m3, m1 = np.meshgrid(
        np.arange(KY) - KY // 2, np.arange(KZ) - KZ // 2, np.arange(KX), indexing="ij"
    )
    m1, m2, m3 = (m.reshape(-1).astype(np.float64) for m in (m1, m2, m3))
    lengths = (
        cell_side_length * total_x,
        cell_side_length * total_y,
        3.0 * cell_side_length * total_z,
    )
    waves = [2.0 * math.pi * m / side for m, side in zip((m1, m2, m3), lengths)]
    squared = sum(k * k for k in waves)
    integer = m1 * m1 + m2 * m2 + m3 * m3
    weight = np.where(
        integer > 0, np.exp(-0.5 * sigma * sigma * squared) / np.maximum(integer, 1.0), 0.0
    ) / math.sqrt(total_x * total_y * total_z * ROWS)
    rows = [weight] + [weight * k for k in waves]
    return np.concatenate([np.stack(rows), np.zeros((4, weight.size))]).astype(np.float32), lengths


def kernel(
    sizes,
    lengths,
    positions,
    species,
    neighbours,
    embed,
    radial_in,
    radial_mid,
    radial_out,
    message,
    mixing,
    update,
    readout_linear,
    readout_hidden,
    readout_out,
    charge_proj,
    waves,
    energy_out,
    force_out,
    pk_src,
    pk_dst,
    oh,
    basis,
    slope,
    pre_one,
    pre_two,
    radial,
    gathered,
    sums,
    geometry,
    state,
    u_src,
    u_ext,
    g_ext,
    g_send,
    g_recv,
    f_ext,
    f_recv,
    plane_buf,
    column_buf,
    phases,
    g_radial,
    g_gathered,
    g_node,
    g_offset,
    send_sem,
    recv_sem,
    plane_send,
    plane_recv,
    column_send,
    column_recv,
):
    nx, ny, nz = sizes
    gx, gy, gz = (lax.axis_index(name) for name in ("gx", "gy", "gz"))
    planes = nx * nz

    def place(c):
        return c // 6, (c // 2) % 3, c % 2

    def exists(c):
        y, x, _ = place(c)
        conditions = []
        if x == 0:
            conditions.append(gx > 0)
        if x == 2:
            conditions.append(gx < nx - 1)
        if y == 0:
            conditions.append(gy > 0)
        if y == 3:
            conditions.append(gy < ny - 1)
        if not conditions:
            return None
        return functools.reduce(jnp.logical_and, conditions)

    def guarded(c, action):
        condition = exists(c)
        if condition is None:
            action()
        else:
            pl.when(condition)(action)

    def device_at(c):
        y, x, o = place(c)
        return (gx + (x - 1), gy + STEP_Y[y], 1 - gz if o else gz)

    def mirror(c):
        y, x, o = place(c)
        return MIRROR_Y[y] * 6 + (2 - x) * 2 + o

    remote = [c for c in range(EXT) if c not in OWN]

    def copy_of(stage, c, source, target):
        return pltpu.make_async_remote_copy(
            src_ref=source(c),
            dst_ref=target(mirror(c)),
            send_sem=send_sem.at[stage, c],
            recv_sem=recv_sem.at[stage, mirror(c)],
            device_id=device_at(c),
            device_id_type=MESH,
        )

    def send(stage, source, target):
        for c in remote:
            guarded(c, lambda c=c: copy_of(stage, c, source, target).start())

    def receive(stage, source, target):
        for c in remote:

            def wait(c=c):
                pltpu.make_async_remote_copy(
                    src_ref=target(c),
                    dst_ref=target(c),
                    send_sem=send_sem.at[stage, mirror(c)],
                    recv_sem=recv_sem.at[stage, c],
                    device_id=device_at(c),
                    device_id_type=MESH,
                ).wait_recv()

            guarded(c, wait)

    def drain(stage, source, target):
        for c in remote:
            guarded(c, lambda c=c: copy_of(stage, c, source, target).wait_send())

    def peer_plane(step):
        rank = lax.rem(gx * nz + gz + step, planes)
        return (rank // nz, gy, lax.rem(rank, nz))

    def peer_column(step):
        return (gx, lax.rem(gy + step, ny), gz)

    pk_dst[...] = jnp.zeros_like(pk_dst)
    u_ext[...] = jnp.zeros_like(u_ext)
    g_recv[...] = jnp.zeros_like(g_recv)
    f_recv[...] = jnp.zeros_like(f_recv)
    for j in range(2):
        tag = (species[0, j] + 1).astype(f32)
        block = jnp.concatenate(
            [positions[:, 0, j, 0, :], tag, jnp.zeros((4, ROWS), f32)], axis=0
        )
        pk_src[j] = block
        pk_dst[OWN[j]] = block

    barrier = pltpu.get_barrier_semaphore()
    greetings = jnp.int32(0)
    for c in remote:
        y, _, _ = place(c)
        if y == 2:
            continue

        guarded(
            c,
            lambda c=c: pl.semaphore_signal(
                barrier, inc=1, device_id=device_at(c), device_id_type=MESH
            ),
        )
        condition = exists(c)
        greetings = greetings + (1 if condition is None else condition.astype(jnp.int32))
    for step in range(1, planes):
        pl.semaphore_signal(barrier, inc=1, device_id=peer_plane(step), device_id_type=MESH)
    for step in range(1, ny):
        pl.semaphore_signal(barrier, inc=1, device_id=peer_column(step), device_id_type=MESH)
    pl.semaphore_wait(barrier, greetings + (planes - 1) + (ny - 1))

    half = lambda c: 0 if c < 12 else 1
    pk_source = lambda c: pk_src.at[half(c)]
    pk_target = lambda c: pk_dst.at[c]
    send(0, pk_source, pk_target)

    near_cells = []
    for j in range(2):
        entry = jnp.concatenate([neighbours[k, 0, j, :, :] for k in range(K)], axis=0)
        code = jnp.right_shift(entry, 7)
        row = jnp.bitwise_and(entry, ROWS - 1)
        third = jnp.right_shift(code * 171, 9)
        shift_x = jnp.right_shift(code * 57, 9)
        shift_y = third - 3 * shift_x
        other = jnp.where(code - 3 * third == 1, 0, 1)
        near = jnp.where(entry >= 0, shift_y * 6 + shift_x * 2 + other, -1)
        near_cells.append((near, row))
        slot = jnp.where(entry >= 0, near * ROWS + row, -1)
        slot_row = jnp.concatenate([slot[k : k + 1] for k in range(K)], axis=1)

        @pl.loop(0, NEAR)
        def _(c, j=j, slot_row=slot_row):
            base = pl.multiple_of(c * ROWS, ROWS)
            local = slot_row - base
            rows = lax.broadcasted_iota(jnp.int32, (ROWS, EDGES), 0)
            oh[j, pl.ds(base, ROWS), :] = jnp.where(rows == local, 1.0, 0.0).astype(bf16)

    kinds = lax.broadcasted_iota(jnp.int32, (NS, ROWS), 0)
    onehot_own = jnp.concatenate(
        [jnp.where(species[0, j] == kinds, 1.0, 0.0) for j in range(2)], axis=1
    )
    initial_own = dot(embed[...], onehot_own.astype(bf16))
    table_one = dot(message[0], embed[...]).astype(bf16)
    ones_row = jnp.ones((1, 2 * ROWS), f32)
    linear = dot(readout_linear[...], ones_row, ((0,), (0,)), HIGH)
    out_weight = dot(readout_out[...], ones_row, ((0,), (0,)), HIGH)

    def mixed(l):
        return dot(mixing[l], onehot_own, precision=HIGH)

    pos_rows = [
        jnp.concatenate([pk_src[j][m : m + 1] for j in range(2)], axis=1) for m in range(3)
    ]
    count = lax.broadcasted_iota(jnp.int32, (8, 2 * ROWS), 0).astype(f32)
    angle_x = count * (pos_rows[0] * (2.0 * math.pi / lengths[0]))
    angle_y = (count - KY // 2) * (pos_rows[1] * (2.0 * math.pi / lengths[1]))
    angle_z = (count - KZ // 2) * (pos_rows[2] * (2.0 * math.pi / lengths[2]))
    cos_x, sin_x = jnp.cos(angle_x), jnp.sin(angle_x)
    cos_y, sin_y = jnp.cos(angle_y), jnp.sin(angle_y)
    cos_z, sin_z = jnp.cos(angle_z), jnp.sin(angle_z)
    for b in range(KY):
        cy, sy = cos_y[b : b + 1], sin_y[b : b + 1]
        cxy = cos_x * cy - sin_x * sy
        sxy = sin_x * cy + cos_x * sy
        for c in range(KZ):
            cz, sz = cos_z[c : c + 1], sin_z[c : c + 1]
            base = (b * KZ + c) * KX
            phases[base : base + KX, :] = cxy * cz - sxy * sz
            phases[256 + base : 256 + base + KX, :] = sxy * cz + cxy * sz

    receive(0, pk_source, pk_target)

    for j in range(2):
        near, row = near_cells[j]
        found = [jnp.zeros((K, ROWS), f32) for _ in range(4)]
        for c in range(NEAR):
            block = pk_dst[j * 6 + c]
            here = near == c
            for m in range(4):
                wide = jnp.broadcast_to(block[m : m + 1], (K, ROWS))
                taken = jnp.take_along_axis(wide, row, axis=1, mode="promise_in_bounds")
                found[m] = jnp.where(here, taken, found[m])
        own = pk_src[j]
        live = near >= 0
        offset = [
            jnp.where(live, found[m] - jnp.broadcast_to(own[m : m + 1], (K, ROWS)), 0.0)
            for m in range(3)
        ]
        squared = offset[0] * offset[0] + offset[1] * offset[1] + offset[2] * offset[2]
        distance = jnp.sqrt(squared + 1.0)
        inverse = 1.0 / distance
        for m in range(3):
            geometry[j, m] = offset[m] * inverse
        geometry[j, 3] = inverse
        reduced = distance * (1.0 / cutoff)
        inside = 1.0 - reduced * reduced
        harmonic = (lax.broadcasted_iota(jnp.int32, (8, ROWS), 0) + 1).astype(f32)
        for k in range(K):
            lanes = slice(k * ROWS, (k + 1) * ROWS)
            red = reduced[k : k + 1]
            ins = inside[k : k + 1]
            env = ins * ins
            angle = harmonic * (red * math.pi)
            sine, cosine = jnp.sin(angle), jnp.cos(angle)
            basis[j, :, lanes] = sine * env
            slope[j, :, lanes] = harmonic * (math.pi / cutoff) * cosine * env + sine * (
                ins * red * (-4.0 / cutoff)
            )
            kind = (kinds + 1).astype(f32)
            hot = jnp.where(found[3][k : k + 1] == kind, 1.0, 0.0).astype(bf16)
            gathered[0, j, :, lanes] = dot(table_one, hot).astype(bf16)

    def radial_net(l):
        for j in range(2):
            first = dot(radial_in[l], basis[j].astype(bf16))
            pre_one[l, j] = first
            hidden = (first * sigmoid(first)).astype(bf16)
            second = dot(radial_mid[l], hidden)
            pre_two[l, j] = second
            hidden = (second * sigmoid(second)).astype(bf16)
            radial[l, j] = dot(radial_out[l], hidden)

    def layer(l, node, mix):
        for j in range(2):
            own_lanes = slice(j * ROWS, (j + 1) * ROWS)
            for b in range(0, C, 32):
                totals = [None] * 4
                for k in range(K):
                    lanes = slice(k * ROWS, (k + 1) * ROWS)
                    u = gathered[l, j, b : b + 32, lanes].astype(f32)
                    vector = radial[l, j, C + b : C + b + 32, lanes] * u
                    terms = [radial[l, j, b : b + 32, lanes] * u] + [
                        vector * geometry[j, m, k : k + 1, :] for m in range(3)
                    ]
                    totals = [t if s is None else s + t for s, t in zip(totals, terms)]
                for m in range(4):
                    sums[l, m, b : b + 32, own_lanes] = totals[m] * (2.0 / K)
        a0, a1, a2, a3 = (sums[l, m] for m in range(4))
        invariant = jnp.concatenate([a0, a1 * a1 + a2 * a2 + a3 * a3, a0 * a0], axis=0)
        weighted = (invariant * mix).astype(bf16)
        return (node + dot(update[l], weighted)).astype(bf16)

    radial_net(0)
    h_one = layer(0, initial_own, mixed(0))
    state[...] = h_one.astype(f32)
    u_two = dot(message[1], h_one).astype(bf16)
    u_src[...] = u_two
    for j in range(2):
        u_ext[:, OWN[j] * ROWS : (OWN[j] + 1) * ROWS] = u_two[:, j * ROWS : (j + 1) * ROWS]
    u_source = lambda c: u_src.at[:, half(c) * ROWS : (half(c) + 1) * ROWS]
    u_target = lambda c: u_ext.at[:, c * ROWS : (c + 1) * ROWS]
    send(1, u_source, u_target)
    radial_net(1)
    receive(1, u_source, u_target)
    for j in range(2):
        start = j * 6 * ROWS
        gathered[1, j] = dot(u_ext[:, start : start + NEAR * ROWS], oh[j]).astype(bf16)
    h_two = layer(1, state[...], mixed(1))

    charge = dot(charge_proj[...], h_two)
    partial = jnp.concatenate(
        [
            dot(charge, phases[:256, :], ((1,), (1,)), HIGH),
            dot(charge, phases[256:, :], ((1,), (1,)), HIGH),
        ],
        axis=0,
    )
    plane_buf[0] = partial

    def plane_copy(step):
        return pltpu.make_async_remote_copy(
            src_ref=plane_buf.at[0],
            dst_ref=plane_buf.at[step],
            send_sem=plane_send.at[step],
            recv_sem=plane_recv.at[step],
            device_id=peer_plane(step),
            device_id_type=MESH,
        )

    def column_copy(step):
        return pltpu.make_async_remote_copy(
            src_ref=column_buf.at[0],
            dst_ref=column_buf.at[step],
            send_sem=column_send.at[step],
            recv_sem=column_recv.at[step],
            device_id=peer_column(step),
            device_id_type=MESH,
        )

    for step in range(1, planes):
        plane_copy(step).start()
    before = dot(readout_hidden[...], h_two)
    gate = sigmoid(before)
    short = jnp.sum(linear * state[...], axis=0, keepdims=True) + jnp.sum(
        out_weight * before * gate, axis=0, keepdims=True
    )
    g_before = out_weight * gate * (1.0 + before * (1.0 - gate))
    g_two = dot(readout_hidden[...], g_before.astype(bf16), ((0,), (0,)))
    for step in range(1, planes):
        plane_copy(step).wait_recv()
    column_buf[0] = jnp.sum(plane_buf[...], axis=0)
    for step in range(1, ny):
        column_copy(step).start()
    for step in range(1, ny):
        column_copy(step).wait_recv()
    structure = jnp.sum(column_buf[...], axis=0)
    s_cos, s_sin = structure[:NQ], structure[NQ:]
    rows = [waves[m : m + 1, :] for m in range(4)]
    with_cos = jnp.concatenate([s_cos * rows[0]] + [s_sin * rows[m] for m in (1, 2, 3)], axis=0)
    with_sin = jnp.concatenate([s_sin * rows[0]] + [-s_cos * rows[m] for m in (1, 2, 3)], axis=0)
    far = dot(with_cos, phases[:256, :], precision=HIGH) + dot(
        with_sin, phases[256:, :], precision=HIGH
    )
    potential = far[:NQ]
    per_atom = short + jnp.sum(charge * potential, axis=0, keepdims=True)
    for j in range(2):
        energy_out[0, j] = per_atom[:, j * ROWS : (j + 1) * ROWS]
    far_force = [
        2.0 * jnp.sum(charge * far[NQ * (m + 1) : NQ * (m + 2)], axis=0, keepdims=True)
        for m in range(3)
    ]
    g_two = g_two + dot(charge_proj[...], (2.0 * potential).astype(bf16), ((0,), (0,)))

    def layer_back(l, grad):
        g_weighted = dot(update[l], grad.astype(bf16), ((0,), (0,))) * mixed(l)
        g_square = 2.0 * g_weighted[C : 2 * C]
        a0 = sums[l, 0]
        g_node[0] = (2.0 / K) * (g_weighted[:C] + 2.0 * a0 * g_weighted[2 * C :])
        for m in range(1, 4):
            g_node[m] = (2.0 / K) * (g_square * sums[l, m])
        for j in range(2):
            own_lanes = slice(j * ROWS, (j + 1) * ROWS)
            g_direction = [[], [], []]
            for k in range(K):
                lanes = slice(k * ROWS, (k + 1) * ROWS)
                directions = [geometry[j, m, k : k + 1, :] for m in range(3)]
                partials = [None] * 3
                for b in range(0, C, 32):
                    u = gathered[l, j, b : b + 32, lanes].astype(f32)
                    g0, g1, g2, g3 = (g_node[m, b : b + 32, own_lanes] for m in range(4))
                    along = g1 * directions[0] + g2 * directions[1] + g3 * directions[2]
                    r_vector = radial[l, j, C + b : C + b + 32, lanes]
                    g_radial[b : b + 32, lanes] = (g0 * u).astype(bf16)
                    g_radial[C + b : C + b + 32, lanes] = (along * u).astype(bf16)
                    if l == 1:
                        r_scalar = radial[l, j, b : b + 32, lanes]
                        g_gathered[b : b + 32, lanes] = (r_scalar * g0 + r_vector * along).astype(
                            bf16
                        )
                    product = r_vector * u
                    for m, g in enumerate((g1, g2, g3)):
                        term = product * g
                        term = (term[0:8] + term[8:16]) + (term[16:24] + term[24:32])
                        partials[m] = term if partials[m] is None else partials[m] + term
                for m in range(3):
                    g_direction[m].append(jnp.sum(partials[m], axis=0, keepdims=True))
            if l == 1:
                scattered = dot(g_gathered[...], oh[j], ((1,), (1,)))
                start = j * 6 * ROWS
                if j == 0:
                    g_ext[:, : NEAR * ROWS] = scattered
                else:
                    g_ext[:, start : NEAR * ROWS] += scattered[:, : NEAR * ROWS - start]
                    g_ext[:, NEAR * ROWS :] = scattered[:, NEAR * ROWS - start :]
            yield j, g_direction

    def radial_back(l, j, g_direction):
        g_hidden = dot(radial_out[l], g_radial[...], ((0,), (0,)))
        second = pre_two[l, j]
        gate = sigmoid(second)
        g_second = g_hidden * (gate * (1.0 + second * (1.0 - gate)))
        g_hidden = dot(radial_mid[l], g_second.astype(bf16), ((0,), (0,)))
        first = pre_one[l, j]
        gate = sigmoid(first)
        g_first = g_hidden * (gate * (1.0 + first * (1.0 - gate)))
        g_basis = dot(radial_in[l], g_first.astype(bf16), ((0,), (0,)))
        g_row = jnp.sum(g_basis * slope[j], axis=0, keepdims=True)
        g_distance = jnp.concatenate(
            [g_row[:, k * ROWS : (k + 1) * ROWS] for k in range(K)], axis=0
        )
        directions = [geometry[j, m] for m in range(3)]
        inverse = geometry[j, 3]
        across = [jnp.concatenate(g_direction[m], axis=0) for m in range(3)]
        along = across[0] * directions[0] + across[1] * directions[1] + across[2] * directions[2]
        radial_part = g_distance - along * inverse
        for m in range(3):
            value = directions[m] * radial_part + across[m] * inverse
            g_offset[j, m] = value if l == 1 else g_offset[j, m] + value

    for j, g_direction in layer_back(1, g_two):
        radial_back(1, j, g_direction)
    g_send[...] = g_ext[...].astype(bf16)
    g_source = lambda c: g_send.at[:, c * ROWS : (c + 1) * ROWS]
    g_target = lambda c: g_recv.at[c]
    send(2, g_source, g_target)
    receive(2, g_source, g_target)
    collected = []
    for j in range(2):
        total = g_ext[:, OWN[j] * ROWS : (OWN[j] + 1) * ROWS]
        for c in range(12 * j, 12 * j + 12):
            if c not in OWN:
                total = total + g_recv[c].astype(f32)
        collected.append(total)
    g_message = jnp.concatenate(collected, axis=1)
    g_one = linear + g_two + dot(message[1], g_message.astype(bf16), ((0,), (0,)))
    for j, g_direction in layer_back(0, g_one):
        radial_back(0, j, g_direction)

    own_terms = []
    for j in range(2):
        values = [g_offset[j, m] for m in range(3)]
        flat = [
            jnp.concatenate([value[k : k + 1] for k in range(K)], axis=1) for value in values
        ]
        packed = jnp.concatenate(flat + [jnp.zeros((5, EDGES), f32)], axis=0)
        high = packed.astype(bf16).astype(f32)
        both = jnp.concatenate([high, packed - high], axis=0).astype(bf16)
        scattered = dot(both, oh[j], ((1,), (1,)))
        scattered = scattered[:8] + scattered[8:]
        start = j * 6 * ROWS
        if j == 0:
            f_ext[:, : NEAR * ROWS] = scattered
        else:
            f_ext[:, start : NEAR * ROWS] += scattered[:, : NEAR * ROWS - start]
            f_ext[:, NEAR * ROWS :] = scattered[:, NEAR * ROWS - start :]
        centre = [jnp.sum(value, axis=0, keepdims=True) for value in values]
        own_lanes = slice(j * ROWS, (j + 1) * ROWS)
        own_terms.append(
            jnp.concatenate(
                [centre[m] - far_force[m][:, own_lanes] for m in range(3)], axis=0
            )
        )
    f_source = lambda c: f_ext.at[:, c * ROWS : (c + 1) * ROWS]
    f_target = lambda c: f_recv.at[c]
    send(3, f_source, f_target)
    receive(3, f_source, f_target)
    for j in range(2):
        total = f_ext[:, OWN[j] * ROWS : (OWN[j] + 1) * ROWS]
        for c in range(12 * j, 12 * j + 12):
            if c not in OWN:
                total = total + f_recv[c]
        force_out[:, 0, j, 0, :] = own_terms[j] - total[:3]

    drain(0, pk_source, pk_target)
    drain(1, u_source, u_target)
    drain(2, g_source, g_target)
    drain(3, f_source, f_target)
    for step in range(1, planes):
        plane_copy(step).wait_send()
    for step in range(1, ny):
        column_copy(step).wait_send()


def local(sizes, *args):
    (positions, species) = args[:2]
    args = list(args)
    nx, ny, nz = sizes
    _, lx, ly, lz, _ = positions.shape
    assert (lx, ly, lz) == (1, 2, 1) and nz == 2
    table, lengths = wave_table(nx * lx, ny * ly, nz * lz)
    args[10] = args[10].reshape(1, -1)
    args[12] = args[12].reshape(1, -1)
    args.append(jnp.asarray(table))
    vmem = pl.BlockSpec(memory_space=pltpu.VMEM)
    scratch = [
        pltpu.VMEM((2, 8, ROWS), f32),
        pltpu.VMEM((EXT, 8, ROWS), f32),
        pltpu.VMEM((2, NEAR * ROWS, EDGES), bf16),
        pltpu.VMEM((2, 8, EDGES), f32),
        pltpu.VMEM((2, 8, EDGES), f32),
        pltpu.VMEM((2, 2, RH, EDGES), f32),
        pltpu.VMEM((2, 2, RH, EDGES), f32),
        pltpu.VMEM((2, 2, 2 * C, EDGES), f32),
        pltpu.VMEM((2, 2, C, EDGES), bf16),
        pltpu.VMEM((2, 4, C, 2 * ROWS), f32),
        pltpu.VMEM((2, 4, K, ROWS), f32),
        pltpu.VMEM((C, 2 * ROWS), f32),
        pltpu.VMEM((C, 2 * ROWS), bf16),
        pltpu.VMEM((C, SLOTS), bf16),
        pltpu.VMEM((C, SLOTS), f32),
        pltpu.VMEM((C, SLOTS), bf16),
        pltpu.VMEM((EXT, C, ROWS), bf16),
        pltpu.VMEM((8, SLOTS), f32),
        pltpu.VMEM((EXT, 8, ROWS), f32),
        pltpu.VMEM((nx * nz, 8, 256), f32),
        pltpu.VMEM((ny, 8, 256), f32),
        pltpu.VMEM((512, 2 * ROWS), f32),
        pltpu.VMEM((2 * C, EDGES), bf16),
        pltpu.VMEM((C, EDGES), bf16),
        pltpu.VMEM((4, C, 2 * ROWS), f32),
        pltpu.VMEM((2, 3, K, ROWS), f32),
        pltpu.SemaphoreType.DMA((4, EXT)),
        pltpu.SemaphoreType.DMA((4, EXT)),
        pltpu.SemaphoreType.DMA((nx * nz,)),
        pltpu.SemaphoreType.DMA((nx * nz,)),
        pltpu.SemaphoreType.DMA((ny,)),
        pltpu.SemaphoreType.DMA((ny,)),
    ]
    return pl.pallas_call(
        functools.partial(kernel, sizes, lengths),
        out_shape=(
            jax.ShapeDtypeStruct(species.shape, f32),
            jax.ShapeDtypeStruct(positions.shape, f32),
        ),
        in_specs=[vmem] * len(args),
        out_specs=(vmem, vmem),
        scratch_shapes=scratch,
        compiler_params=pltpu.CompilerParams(
            collective_id=0, has_side_effects=True, vmem_limit_bytes=48 * 1024 * 1024
        ),
    )(*args)


def solution(mesh):
    sizes = tuple(mesh.shape[name] for name in ("gx", "gy", "gz"))
    grid = P(None, "gx", "gy", "gz", None)
    in_specs = (grid, P("gx", "gy", "gz", None), grid) + (P(),) * 11
    out_specs = (P("gx", "gy", "gz", None), grid)
    return jax.shard_map(
        functools.partial(local, sizes),
        mesh=mesh,
        in_specs=in_specs,
        out_specs=out_specs,
        check_vma=False,
    )
```
